512 devices in a mesh: mem: 8 (over z_hi, x), tile: 64 (over y, z_lo, core).
Axes of the slice: x: 4, y: 4, z: 16 (z_hi: 2, z_lo: 8; z = z_hi * 8 + z_lo), core: 2. Of those that a mesh axis runs over, the one named last changes fastest.
Arguments:
- vector: float32 [2, 64, 64, 256], P(None, 'tile'), may hold values from -6 to 6
- ensemble: bfloat16 [16, 2, 64, 64, 256], P('mem', None, 'tile'), may hold values from -6 to 6
- diffusivity: float32 [2, 64, 64, 256], P(None, 'tile'), may hold values from 0.04 to 0.24
- norm_weight: float32 [64, 64, 256], P('tile'), may hold values from 0.5 to 2
- static_var: float32 [2, 64, 64, 256], P(None, 'tile'), may hold values from 0.2 to 2
Outputs:
- increment: float32 [2, 64, 64, 256], P(None, 'tile')
The draws below stay inside these ranges and needn't reach their ends.
All inputs are finite; a program needn't handle non-finite values.
Results may differ from the reference program's by a relative error of at most 0.0003.
Values sent between devices are 32-bit elements; how exact they have to be, the bound alone decides.
No kernel may reach another device: no remote copies, remote signals or barrier semaphores. Data moves between devices by JAX's collectives and lax.ppermute only.
A program may use at most 64 MiB of HBM per device.

```python
import math
import jax
import jax.numpy as jnp
from jax import lax

TILE_ROWS = 64
TILE_COLS = 256
COL_TILES = 8
SWEEPS = 8
MEMBERS = 16
TILES = 64
ROW_TILES = 8
ROWS = 512
COLS = 2048


def steps_of(rng, dims, cuts, low, top_value):
    level, own = 1.0, jax.random.fold_in(rng, 6)
    for position, parts in cuts:
        heights = jnp.exp(jax.random.uniform(jax.random.fold_in(own, position), (parts,), jnp.float32, low / len(cuts), top_value / len(cuts)))
        level = level * jnp.repeat(heights, dims[position] // parts).reshape([-1 if axis == position else 1 for axis in range(len(dims))])
    return level


def bell_draw(key, dims, spread, most, cuts=(), kind=jnp.bfloat16):
    gain = steps_of(key, dims, cuts, -0.22, 0.18) if cuts else 1.0
    drawn = jax.random.normal(key, dims, jnp.float32) * spread * gain
    return jnp.minimum(jnp.maximum(drawn, -most), most).astype(kind)


def setup_inputs(seed: int = 0) -> dict:
    keys = jax.random.split(jax.random.key(seed), 6)
    return {
        "vector": bell_draw(keys[0], (2, TILES, TILE_ROWS, TILE_COLS), 1.0, 6.0, ((1, 64),), jnp.float32),
        "ensemble": bell_draw(keys[1], (MEMBERS, 2, TILES, TILE_ROWS, TILE_COLS), 1.0, 6.0, ((0, 8), (2, 64))),
        "diffusivity": jnp.clip(0.04 + 0.19999999552965164 * jax.random.uniform(keys[2], (2, TILES, TILE_ROWS, TILE_COLS), jnp.float32) ** steps_of(keys[2], (2, TILES, TILE_ROWS, TILE_COLS), ((1, 64),), -0.2, 0.2), 0.04, 0.24),
        "norm_weight": jnp.clip(jnp.exp(math.log(2.0) - 1.3862944 * jax.random.uniform(keys[3], (TILES, TILE_ROWS, TILE_COLS), jnp.float32) ** steps_of(keys[3], (TILES, TILE_ROWS, TILE_COLS), ((0, 64),), -0.2, 0.2)), 0.5, 2.0),
        "static_var": jnp.clip(jnp.exp(math.log(2.0) - 2.3025851 * jax.random.uniform(keys[4], (2, TILES, TILE_ROWS, TILE_COLS), jnp.float32) ** steps_of(keys[4], (2, TILES, TILE_ROWS, TILE_COLS), ((1, 64),), -0.2, 0.2)), 0.2, 2.0),
    }


ens_weight = 0.7
static_weight = 0.3


def diffuse(values, row_coef, col_coef):
    row_flux = row_coef[:-1, 1:-1] * (values[..., 1:, 1:-1] - values[..., :-1, 1:-1])
    col_flux = col_coef[1:-1, :-1] * (values[..., 1:-1, 1:] - values[..., 1:-1, :-1])
    return (values[..., 1:-1, 1:-1] + row_flux[..., 1:, :] - row_flux[..., :-1, :]
            + col_flux[..., 1:] - col_flux[..., :-1])


def to_slab(tiled):
    lead = tiled.shape[:-3]
    split = tiled.reshape(lead + (ROW_TILES, COL_TILES, TILE_ROWS, TILE_COLS))
    return jnp.swapaxes(split, -3, -2).reshape(lead + (ROWS, COLS))


def to_tiles(slab):
    lead = slab.shape[:-2]
    split = slab.reshape(lead + (ROW_TILES, TILE_ROWS, COL_TILES, TILE_COLS))
    return jnp.swapaxes(split, -3, -2).reshape(lead + (TILES, TILE_ROWS, TILE_COLS))


def reference(vector, ensemble, diffusivity, norm_weight, static_var):
    vec = to_slab(vector)
    weight = to_slab(norm_weight)
    coefs = to_slab(diffusivity)
    row_index = jnp.arange(ROWS)[:, None]
    col_index = jnp.arange(COLS)[None, :]
    row_coef = jnp.where(row_index < ROWS - 1, coefs[0], jnp.float32(0.0))
    col_coef = jnp.where(col_index < COLS - 1, coefs[1], jnp.float32(0.0))
    row_ext = jnp.pad(row_coef, 1)
    col_ext = jnp.pad(col_coef, 1)

    def member_term(running, member):
        pert = to_slab(member).astype(jnp.float32)
        values = weight * pert * vec
        for _ in range(2 * SWEEPS):
            values = diffuse(jnp.pad(values, ((0, 0), (1, 1), (1, 1))), row_ext, col_ext)
        return running + pert * weight * values, None

    total, _ = lax.scan(member_term, jnp.zeros((2, ROWS, COLS), jnp.float32), ensemble)
    ens_part = total / jnp.float32(MEMBERS - 1)
    result = ens_weight * ens_part + static_weight * to_slab(static_var) * vec
    return to_tiles(result)
```

```python
import jax
import jax.numpy as jnp
from jax import lax
from jax.experimental import pallas as pl
from jax.experimental.pallas import tpu as pltpu
from jax.sharding import PartitionSpec as P

COL_TILES = 8
SWEEPS = 8
HALO = 2 * SWEEPS
LANES = 128
FIELDS = 4
TALL = 64 + 2 * HALO
RING = FIELDS * (256 + 2 * HALO)
GROUPS = TALL // 8

ens_weight = 0.7
static_weight = 0.3

F32 = jnp.float32


def masked_coefs(dif_ref, edge_ref):
    nrows, ncols = dif_ref.shape[-2:]
    row = lax.broadcasted_iota(jnp.int32, (nrows, ncols), 0)
    col = lax.broadcasted_iota(jnp.int32, (nrows, ncols), 1)
    row_coef = jnp.where((row == nrows - 1) & (edge_ref[0] == 1), F32(0.0), dif_ref[0])
    col_coef = jnp.where((col == ncols - 1) & (edge_ref[1] == 1), F32(0.0), dif_ref[1])
    return row_coef, col_coef


def own_fields(vec_ref, ens_ref, dif_ref, weight_ref, edge_ref):
    starts = []
    for m in range(2):
        for c in range(2):
            starts.append(weight_ref[...] * ens_ref[m, c].astype(F32) * vec_ref[c])
    return starts + list(masked_coefs(dif_ref, edge_ref))


def row_messages(edge_ref, vec_ref, ens_ref, dif_ref, weight_ref, first_ref, last_ref):
    for k, field in enumerate(own_fields(vec_ref, ens_ref, dif_ref, weight_ref, edge_ref)):
        first_ref[k] = field[:HALO]
        last_ref[k] = field[-HALO:]


def tall_fields(edge_ref, vec_ref, ens_ref, dif_ref, weight_ref, above_ref, below_ref):
    own = own_fields(vec_ref, ens_ref, dif_ref, weight_ref, edge_ref)
    return [jnp.concatenate([above_ref[k], own[k], below_ref[k]], 0) for k in range(6)]


def col_messages(edge_ref, vec_ref, ens_ref, dif_ref, weight_ref, above_ref, below_ref, first_ref, last_ref):
    tall = tall_fields(edge_ref, vec_ref, ens_ref, dif_ref, weight_ref, above_ref, below_ref)
    lane = lax.broadcasted_iota(jnp.int32, (TALL, LANES), 1)
    first = tall[0][:, :LANES]
    last = pltpu.roll(tall[0][:, -LANES:], HALO, 1)
    for k in range(1, 6):
        here = lane >= k * HALO
        first = jnp.where(here, pltpu.roll(tall[k][:, :LANES], k * HALO, 1), first)
        last = jnp.where(here, pltpu.roll(tall[k][:, -LANES:], (k + 1) * HALO, 1), last)
    first_ref[...] = first
    last_ref[...] = last


def sweep(src, dst, row_ref, col_ref, begin, end):
    sub = lax.broadcasted_iota(jnp.int32, (8, RING), 0)
    here = src[8 * begin : 8 * begin + 8, :]
    here_up = pltpu.roll(here, 7, 0)
    flux_above = jnp.zeros((8, RING), F32)
    for g in range(begin, end):
        rows = slice(8 * g, 8 * g + 8)
        if g + 1 < GROUPS:
            after = src[8 * g + 8 : 8 * g + 16, :]
            after_up = pltpu.roll(after, 7, 0)
        else:
            after, after_up = here, here_up
        south = jnp.where(sub == 7, after_up, here_up)
        row_flux = row_ref[rows, :] * (south - here)
        flux_down = pltpu.roll(row_flux, 1, 0)
        north_flux = jnp.where(sub == 0, flux_above, flux_down)
        col_flux = col_ref[rows, :] * (pltpu.roll(here, RING - 1, 1) - here)
        west_flux = pltpu.roll(col_flux, 1, 1)
        dst[rows, :] = here + (row_flux - north_flux) + (col_flux - west_flux)
        here, here_up, flux_above = after, after_up, flux_down


def localize(
    edge_ref, vec_ref, ens_ref, dif_ref, weight_ref, above_ref, below_ref, left_ref, right_ref,
    out_ref, a_ref, b_ref, row_ref, col_ref,
):
    tall = tall_fields(edge_ref, vec_ref, ens_ref, dif_ref, weight_ref, above_ref, below_ref)
    lane = lax.broadcasted_iota(jnp.int32, (TALL, LANES), 1)

    def padded(k):
        right = pltpu.roll(right_ref[...], (LANES - k * HALO) % LANES, 1) if k else right_ref[...]
        left = pltpu.roll(left_ref[...], LANES - (k + 1) * HALO, 1)
        edge = jnp.where(lane < HALO, right, jnp.where(lane >= LANES - HALO, left, F32(0.0)))
        return jnp.concatenate([tall[k], edge], 1)

    def lay(ref, parts):
        for f in range(FIELDS):
            part = parts[f] if f == 0 else pltpu.roll(parts[f], 32 * f, 1)
            base = 256 * f
            if f == 0:
                ref[:, :384] = part
                wrap = part[:, 256:]
            else:
                keep = lane < 32 * f - HALO
                ref[:, base : base + LANES] = jnp.where(keep, tail, part[:, :LANES])
                ref[:, base + LANES : base + 256] = part[:, LANES:256]
            tail = part[:, 256:]
        ref[:, RING - LANES :] = jnp.where(lane < LANES - HALO, tail, wrap)

    lay(a_ref, [padded(f) for f in range(FIELDS)])
    lay(row_ref, [padded(4)] * FIELDS)
    lay(col_ref, [padded(5)] * FIELDS)

    def two(begin, end):
        def body(_, carry):
            sweep(a_ref, b_ref, row_ref, col_ref, begin, end)
            sweep(b_ref, a_ref, row_ref, col_ref, begin, end)
            return carry
        return body

    b_ref[...] = jnp.zeros_like(b_ref)
    lax.fori_loop(0, SWEEPS // 2, two(0, GROUPS), 0)
    lax.fori_loop(0, SWEEPS // 2, two(1, GROUPS - 1), 0)

    for c in range(2):
        total = None
        for m in range(2):
            f = 2 * m + c
            spread = a_ref[HALO:-HALO, 256 * f : 256 * f + 384]
            if f:
                spread = pltpu.roll(spread, 384 - 32 * f, 1)
            term = ens_ref[m, c].astype(F32) * weight_ref[...] * spread[:, :256]
            total = term if total is None else total + term
        for x in range(4):
            out_ref[x, c] = total[16 * x : 16 * x + 16]


def local(vector, ensemble, diffusivity, norm_weight, static_var):
    vec = vector[:, 0]
    weight = norm_weight[0]
    ens = ensemble[:, :, 0]
    dif = diffusivity[:, 0]
    tiles = lax.axis_size("tile")
    row_tiles = tiles // COL_TILES
    tile_id = lax.axis_index("tile")
    edge = jnp.stack(
        [tile_id // COL_TILES == row_tiles - 1, tile_id % COL_TILES == COL_TILES - 1]
    ).astype(jnp.int32)
    vmem = pl.BlockSpec(memory_space=pltpu.VMEM)
    smem = pl.BlockSpec(memory_space=pltpu.SMEM)
    params = pltpu.CompilerParams(vmem_limit_bytes=32 * 2**20)
    own = (edge, vec, ens, dif, weight)
    own_specs = [smem] + [vmem] * 4

    row_msg = jax.ShapeDtypeStruct((6, HALO, 256), F32)
    first, last = pl.pallas_call(
        row_messages, out_shape=(row_msg, row_msg), in_specs=own_specs, out_specs=(vmem, vmem),
        compiler_params=params,
    )(*own)
    down = [(i, i + COL_TILES) for i in range(tiles - COL_TILES)]
    up = [(b, a) for a, b in down]
    above = lax.ppermute(last, "tile", down)
    below = lax.ppermute(first, "tile", up)

    col_msg = jax.ShapeDtypeStruct((TALL, LANES), F32)
    first, last = pl.pallas_call(
        col_messages, out_shape=(col_msg, col_msg), in_specs=own_specs + [vmem] * 2, out_specs=(vmem, vmem),
        compiler_params=params,
    )(*own, above, below)
    rightward = [(i, i + 1) for i in range(tiles) if (i + 1) % COL_TILES]
    leftward = [(b, a) for a, b in rightward]
    left = lax.ppermute(last, "tile", rightward)
    right = lax.ppermute(first, "tile", leftward)

    partial = pl.pallas_call(
        localize,
        out_shape=jax.ShapeDtypeStruct((4, 2, 16, 256), F32),
        in_specs=own_specs + [vmem] * 4,
        out_specs=vmem,
        scratch_shapes=[pltpu.VMEM((TALL, RING), F32)] * 4,
        compiler_params=params,
    )(*own, above, below, left, right)

    along_x = [[0, 1, 2, 3], [4, 5, 6, 7]]
    parts = lax.all_to_all(partial, "mem", 0, 0, axis_index_groups=along_x, tiled=True)
    mine = jnp.sum(parts, 0)
    other = lax.ppermute(mine, "mem", [(i, (i + 4) % 8) for i in range(8)])
    both = jnp.broadcast_to((mine + other)[None], (4, 2, 16, 256))
    summed = lax.all_to_all(both, "mem", 0, 0, axis_index_groups=along_x, tiled=True)
    summed = jnp.swapaxes(summed, 0, 1).reshape(2, 64, 256)
    members = lax.axis_size("mem") * ensemble.shape[0]
    ens_part = summed / F32(members - 1)
    result = ens_weight * ens_part + static_weight * static_var[:, 0] * vec
    return result[:, None]


def solution(mesh):
    placed = (
        P(None, "tile", None, None),
        P("mem", None, "tile", None, None),
        P(None, "tile", None, None),
        P("tile", None, None),
        P(None, "tile", None, None),
    )
    return jax.shard_map(
        local, mesh=mesh, in_specs=placed, out_specs=P(None, "tile", None, None), check_vma=False
    )
```

```python
import jax
import jax.numpy as jnp
from jax import lax
from jax.experimental import pallas as pl
from jax.experimental.pallas import tpu as pltpu
from jax.sharding import PartitionSpec as P

COL_TILES = 8
SWEEPS = 8
HALO = 2 * SWEEPS
LANES = 128
FIELDS = 4
TALL = 64 + 2 * HALO
RING = FIELDS * (256 + 2 * HALO)
GROUPS = TALL // 8

ens_weight = 0.7
static_weight = 0.3

F32 = jnp.float32


def fetch(pairs, sems):
    copies = [pltpu.make_async_copy(src, dst, sems.at[i]) for i, (src, dst) in enumerate(pairs)]
    for copy in copies:
        copy.start()
    for copy in copies:
        copy.wait()


def row_messages(edge_ref, vec_hbm, ens_hbm, dif_hbm, weight_hbm, first_ref, last_ref, vec, ens, dif, weight, sems):
    nrows = vec_hbm.shape[2]
    pairs = []
    for side, begin in enumerate((0, nrows - HALO)):
        rows = pl.ds(begin, HALO)
        pairs += [
            (vec_hbm.at[:, 0, rows, :], vec.at[side]),
            (ens_hbm.at[:, :, 0, rows, :], ens.at[side]),
            (dif_hbm.at[:, 0, rows, :], dif.at[side]),
            (weight_hbm.at[0, rows, :], weight.at[side]),
        ]
    fetch(pairs, sems)
    row = lax.broadcasted_iota(jnp.int32, (HALO, 256), 0)
    col = lax.broadcasted_iota(jnp.int32, (HALO, 256), 1)
    for side, ref in enumerate((first_ref, last_ref)):
        for m in range(2):
            for c in range(2):
                ref[2 * m + c] = weight[side] * ens[side, m, c].astype(F32) * vec[side, c]
        row_coef, col_coef = dif[side, 0], dif[side, 1]
        if side == 1:
            row_coef = jnp.where((row == HALO - 1) & (edge_ref[0] == 1), F32(0.0), row_coef)
        ref[4] = row_coef
        ref[5] = jnp.where((col == 255) & (edge_ref[1] == 1), F32(0.0), col_coef)


def pack_cols(fields):
    lane = lax.broadcasted_iota(jnp.int32, (fields[0].shape[0], LANES), 1)
    first = fields[0][:, :LANES]
    last = pltpu.roll(fields[0][:, -LANES:], HALO, 1)
    for k in range(1, 6):
        here = lane >= k * HALO
        first = jnp.where(here, pltpu.roll(fields[k][:, :LANES], k * HALO, 1), first)
        last = jnp.where(here, pltpu.roll(fields[k][:, -LANES:], (k + 1) * HALO, 1), last)
    return first, last


def own_arrays(
    edge_ref, vec_hbm, ens_hbm, dif_hbm, weight_hbm, var_hbm, sent_hbm,
    own_ref, scale_ref, fixed_ref, first_ref, last_ref, vec, ens, dif, weight, var, sems,
):
    fetch(
        [
            (vec_hbm.at[:, 0], vec), (ens_hbm.at[:, :, 0], ens), (dif_hbm.at[:, 0], dif),
            (weight_hbm.at[0], weight), (var_hbm.at[:, 0], var),
        ],
        sems,
    )
    nrows, ncols = weight.shape
    for m in range(2):
        for c in range(2):
            scale = weight[...] * ens[m, c].astype(F32)
            scale_ref[2 * m + c] = scale
            own_ref[2 * m + c] = scale * vec[c]
    row = lax.broadcasted_iota(jnp.int32, (nrows, ncols), 0)
    col = lax.broadcasted_iota(jnp.int32, (nrows, ncols), 1)
    own_ref[4] = jnp.where((row == nrows - 1) & (edge_ref[0] == 1), F32(0.0), dif[0])
    own_ref[5] = jnp.where((col == ncols - 1) & (edge_ref[1] == 1), F32(0.0), dif[1])
    for c in range(2):
        fixed_ref[c] = F32(static_weight) * var[c] * vec[c]
    first_ref[...], last_ref[...] = pack_cols([own_ref[k] for k in range(6)])


def col_messages(first_own, last_own, above_ref, below_ref, first_ref, last_ref):
    for rows, ref in ((slice(0, HALO), above_ref), (slice(TALL - HALO, TALL), below_ref)):
        first_ref[rows, :], last_ref[rows, :] = pack_cols([ref[k] for k in range(6)])
    first_ref[HALO:-HALO, :] = first_own[...]
    last_ref[HALO:-HALO, :] = last_own[...]


PAD = 8
COLUMNS = RING // LANES


def sweep(src, dst, row_ref, col_ref, west_ref, begin, end):
    lane = lax.broadcasted_iota(jnp.int32, (8, LANES), 1)

    def turned(g):
        p = PAD + 8 * g
        here = [src[j, p : p + 8, :] for j in range(COLUMNS)]
        return here, [pltpu.roll(x, LANES - 1, 1) for x in here], [pltpu.roll(x, 1, 1) for x in here]

    ready = turned(begin)
    for g in range(begin, end):
        here, from_east, from_west = ready
        if g + 1 < end:
            ready = turned(g + 1)
        p = PAD + 8 * g
        for j in range(COLUMNS):
            x = here[j]
            east = jnp.where(lane == LANES - 1, from_east[(j + 1) % COLUMNS], from_east[j])
            west = jnp.where(lane == 0, from_west[j - 1], from_west[j])
            south, north = src[j, p + 1 : p + 9, :], src[j, p - 1 : p + 7, :]
            rows = row_ref[j, p : p + 8, :] * (south - x) - row_ref[j, p - 1 : p + 7, :] * (x - north)
            cols = col_ref[j, p : p + 8, :] * (east - x) - west_ref[j, p : p + 8, :] * (x - west)
            dst[j, p : p + 8, :] = x + rows + cols


def localize(
    own_ref, scale_ref, above_ref, below_ref, left_ref, right_ref,
    out_ref, a_ref, b_ref, row_ref, col_ref, west_ref,
):
    lane = lax.broadcasted_iota(jnp.int32, (TALL, LANES), 1)
    tall = slice(PAD, PAD + TALL)

    def padded(k):
        right = pltpu.roll(right_ref[...], (LANES - k * HALO) % LANES, 1) if k else right_ref[...]
        left = pltpu.roll(left_ref[...], LANES - (k + 1) * HALO, 1)
        edge = jnp.where(lane < HALO, right, jnp.where(lane >= LANES - HALO, left, F32(0.0)))
        return jnp.concatenate([jnp.concatenate([above_ref[k], own_ref[k], below_ref[k]], 0), edge], 1)

    def lay(ref, parts):
        for f in range(FIELDS):
            part = pltpu.roll(parts[f], 32 * f, 1) if f else parts[f]
            if f:
                ref[2 * f, tall, :] = jnp.where(lane < 32 * f - HALO, tail, part[:, :LANES])
            else:
                ref[0, tall, :] = part[:, :LANES]
                wrap = part[:, 256:]
            ref[2 * f + 1, tall, :] = part[:, LANES:256]
            tail = part[:, 256:]
        ref[COLUMNS - 1, tall, :] = jnp.where(lane < LANES - HALO, tail, wrap)

    for ref in (a_ref, b_ref, row_ref):
        ref[:, :PAD, :] = jnp.zeros((COLUMNS, PAD, LANES), F32)
        ref[:, PAD + TALL :, :] = jnp.zeros((COLUMNS, PAD, LANES), F32)
    lay(a_ref, [padded(f) for f in range(FIELDS)])
    lay(row_ref, [padded(4)] * FIELDS)
    lay(col_ref, [padded(5)] * FIELDS)
    for j in range(COLUMNS):
        before = pltpu.roll(col_ref[(j - 1) % COLUMNS, tall, :], 1, 1)
        west_ref[j, tall, :] = jnp.where(lane == 0, before, pltpu.roll(col_ref[j, tall, :], 1, 1))

    def two(begin, end):
        def body(_, carry):
            sweep(a_ref, b_ref, row_ref, col_ref, west_ref, begin, end)
            sweep(b_ref, a_ref, row_ref, col_ref, west_ref, begin, end)
            return carry
        return body

    lax.fori_loop(0, SWEEPS // 2, two(0, GROUPS), 0)
    lax.fori_loop(0, SWEEPS // 2, two(1, GROUPS - 1), 0)

    inner = slice(PAD + HALO, PAD + TALL - HALO)
    for c in range(2):
        total = None
        for m in range(2):
            f = 2 * m + c
            spread = jnp.concatenate([a_ref[2 * f + i, inner, :] for i in range(3)], 1)
            if f:
                spread = pltpu.roll(spread, 384 - 32 * f, 1)
            term = scale_ref[f] * spread[:, :256]
            total = term if total is None else total + term
        out_ref[2 * c] = total[:32]
        out_ref[2 * c + 1] = total[32:]


def local(vector, ensemble, diffusivity, norm_weight, static_var):
    tiles = lax.axis_size("tile")
    row_tiles = tiles // COL_TILES
    tile_id = lax.axis_index("tile")
    edge = jnp.stack(
        [tile_id // COL_TILES == row_tiles - 1, tile_id % COL_TILES == COL_TILES - 1]
    ).astype(jnp.int32)
    vmem = pl.BlockSpec(memory_space=pltpu.VMEM)
    smem = pl.BlockSpec(memory_space=pltpu.SMEM)
    hbm = pl.BlockSpec(memory_space=pltpu.HBM)
    params = pltpu.CompilerParams(vmem_limit_bytes=32 * 2**20)

    def f32(*shape):
        return jax.ShapeDtypeStruct(shape, F32)

    def buffers(*lead, rows):
        return [
            pltpu.VMEM((*lead, 2, rows, 256), F32), pltpu.VMEM((*lead, 2, 2, rows, 256), jnp.bfloat16),
            pltpu.VMEM((*lead, 2, rows, 256), F32), pltpu.VMEM((*lead, rows, 256), F32),
        ]

    held = [
        pltpu.with_memory_space_constraint(x, pltpu.HBM)
        for x in (vector, ensemble, diffusivity, norm_weight, static_var)
    ]
    first, last = pl.pallas_call(
        row_messages, out_shape=(f32(6, HALO, 256),) * 2, in_specs=[smem] + [hbm] * 4, out_specs=(vmem,) * 2,
        scratch_shapes=buffers(2, rows=HALO) + [pltpu.SemaphoreType.DMA((8,))],
        compiler_params=params,
    )(edge, *held[:4])
    down = [(i, i + COL_TILES) for i in range(tiles - COL_TILES)]
    up = [(b, a) for a, b in down]
    above = lax.ppermute(last, "tile", down)
    below = lax.ppermute(first, "tile", up)

    own, scale, fixed, first_own, last_own = pl.pallas_call(
        own_arrays,
        out_shape=(f32(6, 64, 256), f32(4, 64, 256), f32(2, 64, 256), f32(64, LANES), f32(64, LANES)),
        in_specs=[smem] + [hbm] * 6, out_specs=(vmem,) * 5,
        scratch_shapes=buffers(rows=64) + [pltpu.VMEM((2, 64, 256), F32), pltpu.SemaphoreType.DMA((5,))],
        compiler_params=params,
        cost_estimate=pl.CostEstimate(flops=2 * 10**6, bytes_accessed=2 * 10**6, transcendentals=0),
    )(edge, *held, first)

    first, last = pl.pallas_call(
        col_messages, out_shape=(f32(TALL, LANES),) * 2, in_specs=[vmem] * 4, out_specs=(vmem,) * 2,
        compiler_params=params,
    )(first_own, last_own, above, below)
    rightward = [(i, i + 1) for i in range(tiles) if (i + 1) % COL_TILES]
    leftward = [(b, a) for a, b in rightward]
    left = lax.ppermute(last, "tile", rightward)
    right = lax.ppermute(first, "tile", leftward)

    partial = pl.pallas_call(
        localize,
        out_shape=f32(4, 32, 256),
        in_specs=[vmem] * 6,
        out_specs=vmem,
        scratch_shapes=[pltpu.VMEM((COLUMNS, TALL + 2 * PAD, LANES), F32)] * 5,
        compiler_params=params,
    )(own, scale, above, below, left, right)

    along_x = [[0, 1, 2, 3], [4, 5, 6, 7]]
    parts = lax.all_to_all(partial, "mem", 0, 0, axis_index_groups=along_x, tiled=True)
    mine = jnp.sum(parts, 0)
    other = lax.ppermute(mine, "mem", [(i, (i + 4) % 8) for i in range(8)])
    both = jnp.broadcast_to((mine + other)[None], (4, 32, 256))
    summed = lax.all_to_all(both, "mem", 0, 0, axis_index_groups=along_x, tiled=True)
    members = lax.axis_size("mem") * ensemble.shape[0]
    ens_part = summed.reshape(2, 64, 256) / F32(members - 1)
    result = ens_weight * ens_part + fixed
    return result[:, None]


def solution(mesh):
    placed = (
        P(None, "tile", None, None),
        P("mem", None, "tile", None, None),
        P(None, "tile", None, None),
        P("tile", None, None),
        P(None, "tile", None, None),
    )
    return jax.shard_map(
        local, mesh=mesh, in_specs=placed, out_specs=P(None, "tile", None, None), check_vma=False
    )
```

```python
import jax
import jax.numpy as jnp
from jax import lax
from jax.experimental import pallas as pl
from jax.experimental.pallas import tpu as pltpu
from jax.sharding import PartitionSpec as P

COL_TILES = 8
SWEEPS = 8
HALO = 2 * SWEEPS
LANES = 128
FIELDS = 4
TALL = 64 + 2 * HALO
RING = FIELDS * (256 + 2 * HALO)
GROUPS = TALL // 8

ens_weight = 0.7
static_weight = 0.3

F32 = jnp.float32


def at_edges():
    tile_id, tiles = lax.axis_index("tile"), lax.axis_size("tile")
    return tile_id >= tiles - COL_TILES, tile_id % COL_TILES == COL_TILES - 1


def fetch(pairs, sems):
    copies = [pltpu.make_async_copy(src, dst, sems.at[i]) for i, (src, dst) in enumerate(pairs)]
    for copy in copies:
        copy.start()
    for copy in copies:
        copy.wait()


def row_messages(vec_hbm, ens_hbm, dif_hbm, weight_hbm, first_ref, last_ref, vec, ens, dif, weight, sems):
    nrows = vec_hbm.shape[2]
    pairs = []
    for side, begin in enumerate((0, nrows - HALO)):
        rows = pl.ds(begin, HALO)
        pairs += [
            (vec_hbm.at[:, 0, rows, :], vec.at[side]),
            (ens_hbm.at[:, :, 0, rows, :], ens.at[side]),
            (dif_hbm.at[:, 0, rows, :], dif.at[side]),
            (weight_hbm.at[0, rows, :], weight.at[side]),
        ]
    fetch(pairs, sems)
    bottom, rightmost = at_edges()
    row = lax.broadcasted_iota(jnp.int32, (HALO, 256), 0)
    col = lax.broadcasted_iota(jnp.int32, (HALO, 256), 1)
    for side, ref in enumerate((first_ref, last_ref)):
        for m in range(2):
            for c in range(2):
                ref[2 * m + c] = weight[side] * ens[side, m, c].astype(F32) * vec[side, c]
        row_coef, col_coef = dif[side, 0], dif[side, 1]
        if side == 1:
            row_coef = jnp.where((row == HALO - 1) & (bottom), F32(0.0), row_coef)
        ref[4] = row_coef
        ref[5] = jnp.where((col == 255) & (rightmost), F32(0.0), col_coef)


def pack_cols(fields):
    lane = lax.broadcasted_iota(jnp.int32, (fields[0].shape[0], LANES), 1)
    first = fields[0][:, :LANES]
    last = pltpu.roll(fields[0][:, -LANES:], HALO, 1)
    for k in range(1, 6):
        here = lane >= k * HALO
        first = jnp.where(here, pltpu.roll(fields[k][:, :LANES], k * HALO, 1), first)
        last = jnp.where(here, pltpu.roll(fields[k][:, -LANES:], (k + 1) * HALO, 1), last)
    return first, last


def own_arrays(
    vec_hbm, ens_hbm, dif_hbm, weight_hbm, var_hbm, sent_hbm,
    own_ref, scale_ref, fixed_ref, first_ref, last_ref, vec, ens, dif, weight, var, sems,
):
    fetch(
        [
            (vec_hbm.at[:, 0], vec), (ens_hbm.at[:, :, 0], ens), (dif_hbm.at[:, 0], dif),
            (weight_hbm.at[0], weight), (var_hbm.at[:, 0], var),
        ],
        sems,
    )
    nrows, ncols = weight.shape
    bottom, rightmost = at_edges()
    for m in range(2):
        for c in range(2):
            scale = weight[...] * ens[m, c].astype(F32)
            scale_ref[2 * m + c] = scale
            own_ref[2 * m + c] = scale * vec[c]
    row = lax.broadcasted_iota(jnp.int32, (nrows, ncols), 0)
    col = lax.broadcasted_iota(jnp.int32, (nrows, ncols), 1)
    own_ref[4] = jnp.where((row == nrows - 1) & (bottom), F32(0.0), dif[0])
    own_ref[5] = jnp.where((col == ncols - 1) & (rightmost), F32(0.0), dif[1])
    for c in range(2):
        fixed_ref[c] = F32(static_weight) * var[c] * vec[c]
    first_ref[...], last_ref[...] = pack_cols([own_ref[k] for k in range(6)])


def col_messages(first_own, last_own, above_ref, below_ref, first_ref, last_ref):
    for rows, ref in ((slice(0, HALO), above_ref), (slice(TALL - HALO, TALL), below_ref)):
        first_ref[rows, :], last_ref[rows, :] = pack_cols([ref[k] for k in range(6)])
    first_ref[HALO:-HALO, :] = first_own[...]
    last_ref[HALO:-HALO, :] = last_own[...]


PAD = 8
COLUMNS = RING // LANES


def sweep(src, dst, row_ref, col_ref, west_ref, begin, end):
    lane = lax.broadcasted_iota(jnp.int32, (8, LANES), 1)

    def turned(g):
        p = PAD + 8 * g
        here = [src[j, p : p + 8, :] for j in range(COLUMNS)]
        return here, [pltpu.roll(x, LANES - 1, 1) for x in here], [pltpu.roll(x, 1, 1) for x in here]

    ready = turned(begin)
    for g in range(begin, end):
        here, from_east, from_west = ready
        if g + 1 < end:
            ready = turned(g + 1)
        p = PAD + 8 * g
        for j in range(COLUMNS):
            x = here[j]
            east = jnp.where(lane == LANES - 1, from_east[(j + 1) % COLUMNS], from_east[j])
            west = jnp.where(lane == 0, from_west[j - 1], from_west[j])
            south, north = src[j, p + 1 : p + 9, :], src[j, p - 1 : p + 7, :]
            rows = row_ref[j, p : p + 8, :] * (south - x) - row_ref[j, p - 1 : p + 7, :] * (x - north)
            cols = col_ref[j, p : p + 8, :] * (east - x) - west_ref[j, p : p + 8, :] * (x - west)
            dst[j, p : p + 8, :] = x + rows + cols


def localize(
    own_ref, scale_ref, above_ref, below_ref, left_ref, right_ref,
    out_ref, a_ref, b_ref, row_ref, col_ref, west_ref,
):
    lane = lax.broadcasted_iota(jnp.int32, (TALL, LANES), 1)
    tall = slice(PAD, PAD + TALL)

    def padded(k):
        right = pltpu.roll(right_ref[...], (LANES - k * HALO) % LANES, 1) if k else right_ref[...]
        left = pltpu.roll(left_ref[...], LANES - (k + 1) * HALO, 1)
        edge = jnp.where(lane < HALO, right, jnp.where(lane >= LANES - HALO, left, F32(0.0)))
        return jnp.concatenate([jnp.concatenate([above_ref[k], own_ref[k], below_ref[k]], 0), edge], 1)

    def lay(ref, parts):
        for f in range(FIELDS):
            part = pltpu.roll(parts[f], 32 * f, 1) if f else parts[f]
            if f:
                ref[2 * f, tall, :] = jnp.where(lane < 32 * f - HALO, tail, part[:, :LANES])
            else:
                ref[0, tall, :] = part[:, :LANES]
                wrap = part[:, 256:]
            ref[2 * f + 1, tall, :] = part[:, LANES:256]
            tail = part[:, 256:]
        ref[COLUMNS - 1, tall, :] = jnp.where(lane < LANES - HALO, tail, wrap)

    for ref in (a_ref, b_ref, row_ref):
        ref[:, :PAD, :] = jnp.zeros((COLUMNS, PAD, LANES), F32)
        ref[:, PAD + TALL :, :] = jnp.zeros((COLUMNS, PAD, LANES), F32)
    lay(a_ref, [padded(f) for f in range(FIELDS)])
    lay(row_ref, [padded(4)] * FIELDS)
    lay(col_ref, [padded(5)] * FIELDS)
    for j in range(COLUMNS):
        before = pltpu.roll(col_ref[(j - 1) % COLUMNS, tall, :], 1, 1)
        west_ref[j, tall, :] = jnp.where(lane == 0, before, pltpu.roll(col_ref[j, tall, :], 1, 1))

    def two(begin, end):
        def body(_, carry):
            sweep(a_ref, b_ref, row_ref, col_ref, west_ref, begin, end)
            sweep(b_ref, a_ref, row_ref, col_ref, west_ref, begin, end)
            return carry
        return body

    lax.fori_loop(0, SWEEPS // 2, two(0, GROUPS), 0)
    lax.fori_loop(0, SWEEPS // 2, two(1, GROUPS - 1), 0)

    inner = slice(PAD + HALO, PAD + TALL - HALO)
    for c in range(2):
        total = None
        for m in range(2):
            f = 2 * m + c
            spread = jnp.concatenate([a_ref[2 * f + i, inner, :] for i in range(3)], 1)
            if f:
                spread = pltpu.roll(spread, 384 - 32 * f, 1)
            term = scale_ref[f] * spread[:, :256]
            total = term if total is None else total + term
        out_ref[2 * c] = total[:32]
        out_ref[2 * c + 1] = total[32:]


def local(vector, ensemble, diffusivity, norm_weight, static_var):
    tiles = lax.axis_size("tile")
    vmem = pl.BlockSpec(memory_space=pltpu.VMEM)
    hbm = pl.BlockSpec(memory_space=pltpu.HBM)
    params = pltpu.CompilerParams(vmem_limit_bytes=32 * 2**20)

    def f32(*shape):
        return jax.ShapeDtypeStruct(shape, F32)

    def buffers(*lead, rows):
        return [
            pltpu.VMEM((*lead, 2, rows, 256), F32), pltpu.VMEM((*lead, 2, 2, rows, 256), jnp.bfloat16),
            pltpu.VMEM((*lead, 2, rows, 256), F32), pltpu.VMEM((*lead, rows, 256), F32),
        ]

    held = [
        pltpu.with_memory_space_constraint(x, pltpu.HBM)
        for x in (vector, ensemble, diffusivity, norm_weight, static_var)
    ]
    first, last = pl.pallas_call(
        row_messages, out_shape=(f32(6, HALO, 256),) * 2, in_specs=[hbm] * 4, out_specs=(vmem,) * 2,
        scratch_shapes=buffers(2, rows=HALO) + [pltpu.SemaphoreType.DMA((8,))],
        compiler_params=params,
    )(*held[:4])
    down = [(i, i + COL_TILES) for i in range(tiles - COL_TILES)]
    up = [(b, a) for a, b in down]
    above = lax.ppermute(last, "tile", down)
    below = lax.ppermute(first, "tile", up)

    own, scale, fixed, first_own, last_own = pl.pallas_call(
        own_arrays,
        out_shape=(f32(6, 64, 256), f32(4, 64, 256), f32(2, 64, 256), f32(64, LANES), f32(64, LANES)),
        in_specs=[hbm] * 6, out_specs=(vmem,) * 5,
        scratch_shapes=buffers(rows=64) + [pltpu.VMEM((2, 64, 256), F32), pltpu.SemaphoreType.DMA((5,))],
        compiler_params=params,
        cost_estimate=pl.CostEstimate(flops=2 * 10**6, bytes_accessed=2 * 10**6, transcendentals=0),
    )(*held, first)

    first, last = pl.pallas_call(
        col_messages, out_shape=(f32(TALL, LANES),) * 2, in_specs=[vmem] * 4, out_specs=(vmem,) * 2,
        compiler_params=params,
    )(first_own, last_own, above, below)
    rightward = [(i, i + 1) for i in range(tiles) if (i + 1) % COL_TILES]
    leftward = [(b, a) for a, b in rightward]
    left = lax.ppermute(last, "tile", rightward)
    right = lax.ppermute(first, "tile", leftward)

    partial = pl.pallas_call(
        localize,
        out_shape=f32(4, 32, 256),
        in_specs=[vmem] * 6,
        out_specs=vmem,
        scratch_shapes=[pltpu.VMEM((COLUMNS, TALL + 2 * PAD, LANES), F32)] * 5,
        compiler_params=params,
    )(own, scale, above, below, left, right)

    along_x = [[0, 1, 2, 3], [4, 5, 6, 7]]
    parts = lax.all_to_all(partial, "mem", 0, 0, axis_index_groups=along_x, tiled=True)
    mine = jnp.sum(parts, 0)
    pair = lax.all_gather(mine, "mem", axis_index_groups=[[0, 4], [1, 5], [2, 6], [3, 7]])
    both = jnp.broadcast_to((pair[0] + pair[1])[None], (4, 32, 256))
    summed = lax.all_to_all(both, "mem", 0, 0, axis_index_groups=along_x, tiled=True)
    members = lax.axis_size("mem") * ensemble.shape[0]
    ens_part = summed.reshape(2, 64, 256) / F32(members - 1)
    result = ens_weight * ens_part + fixed
    return result[:, None]


def solution(mesh):
    placed = (
        P(None, "tile", None, None),
        P("mem", None, "tile", None, None),
        P(None, "tile", None, None),
        P("tile", None, None),
        P(None, "tile", None, None),
    )
    return jax.shard_map(
        local, mesh=mesh, in_specs=placed, out_specs=P(None, "tile", None, None), check_vma=False
    )
```

```python
import jax
import jax.numpy as jnp
from jax import lax
from jax.experimental import pallas as pl
from jax.experimental.pallas import tpu as pltpu
from jax.sharding import PartitionSpec as P

COL_TILES = 8
SWEEPS = 8
HALO = 2 * SWEEPS
LANES = 128
FIELDS = 4
TALL = 64 + 2 * HALO
RING = FIELDS * (256 + 2 * HALO)
GROUPS = TALL // 8

ens_weight = 0.7
static_weight = 0.3

F32 = jnp.float32


def at_edges():
    tile_id, tiles = lax.axis_index("tile"), lax.axis_size("tile")
    return tile_id >= tiles - COL_TILES, tile_id % COL_TILES == COL_TILES - 1


def fetch(pairs, sems):
    copies = [pltpu.make_async_copy(src, dst, sems.at[i]) for i, (src, dst) in enumerate(pairs)]
    for copy in copies:
        copy.start()
    for copy in copies:
        copy.wait()


def row_messages(vec_hbm, ens_hbm, dif_hbm, weight_hbm, first_ref, last_ref, vec, ens, dif, weight, sems):
    nrows = vec_hbm.shape[2]
    pairs = []
    for side, begin in enumerate((0, nrows - HALO)):
        rows = pl.ds(begin, HALO)
        pairs += [
            (vec_hbm.at[:, 0, rows, :], vec.at[side]),
            (ens_hbm.at[:, :, 0, rows, :], ens.at[side]),
            (dif_hbm.at[:, 0, rows, :], dif.at[side]),
            (weight_hbm.at[0, rows, :], weight.at[side]),
        ]
    fetch(pairs, sems)
    bottom, rightmost = at_edges()
    row = lax.broadcasted_iota(jnp.int32, (HALO, 256), 0)
    col = lax.broadcasted_iota(jnp.int32, (HALO, 256), 1)
    for side, ref in enumerate((first_ref, last_ref)):
        for m in range(2):
            for c in range(2):
                ref[2 * m + c] = weight[side] * ens[side, m, c].astype(F32) * vec[side, c]
        row_coef, col_coef = dif[side, 0], dif[side, 1]
        if side == 1:
            row_coef = jnp.where((row == HALO - 1) & (bottom), F32(0.0), row_coef)
        ref[4] = row_coef
        ref[5] = jnp.where((col == 255) & (rightmost), F32(0.0), col_coef)


def pack_cols(fields):
    lane = lax.broadcasted_iota(jnp.int32, (fields[0].shape[0], LANES), 1)
    first = fields[0][:, :LANES]
    last = pltpu.roll(fields[0][:, -LANES:], HALO, 1)
    for k in range(1, 6):
        here = lane >= k * HALO
        first = jnp.where(here, pltpu.roll(fields[k][:, :LANES], k * HALO, 1), first)
        last = jnp.where(here, pltpu.roll(fields[k][:, -LANES:], (k + 1) * HALO, 1), last)
    return first, last


def own_arrays(
    vec_hbm, ens_hbm, dif_hbm, weight_hbm, var_hbm, sent_hbm,
    own_ref, scale_ref, fixed_ref, first_ref, last_ref, vec, ens, dif, weight, var, sems,
):
    fetch(
        [
            (vec_hbm.at[:, 0], vec), (ens_hbm.at[:, :, 0], ens), (dif_hbm.at[:, 0], dif),
            (weight_hbm.at[0], weight), (var_hbm.at[:, 0], var),
        ],
        sems,
    )
    nrows, ncols = weight.shape
    bottom, rightmost = at_edges()
    for m in range(2):
        for c in range(2):
            scale = weight[...] * ens[m, c].astype(F32)
            scale_ref[2 * m + c] = scale
            own_ref[2 * m + c] = scale * vec[c]
    row = lax.broadcasted_iota(jnp.int32, (nrows, ncols), 0)
    col = lax.broadcasted_iota(jnp.int32, (nrows, ncols), 1)
    own_ref[4] = jnp.where((row == nrows - 1) & (bottom), F32(0.0), dif[0])
    own_ref[5] = jnp.where((col == ncols - 1) & (rightmost), F32(0.0), dif[1])
    for c in range(2):
        fixed_ref[c] = F32(static_weight) * var[c] * vec[c]
    first_ref[...], last_ref[...] = pack_cols([own_ref[k] for k in range(6)])


def corner_messages(above_ref, below_ref, sent_ref, first_ref, last_ref):
    for side, ref in enumerate((above_ref, below_ref)):
        rows = slice(HALO * side, HALO * side + HALO)
        first_ref[rows, :], last_ref[rows, :] = pack_cols([ref[k] for k in range(6)])


EARLY = 4
PAD = 8
COLUMNS = RING // LANES


def sweep(src, dst, row_ref, col_ref, west_ref, begin, end):
    lane = lax.broadcasted_iota(jnp.int32, (8, LANES), 1)

    def turned(g):
        p = PAD + 8 * g
        here = [src[j, p : p + 8, :] for j in range(COLUMNS)]
        return here, [pltpu.roll(x, LANES - 1, 1) for x in here], [pltpu.roll(x, 1, 1) for x in here]

    ready = turned(begin)
    for g in range(begin, end):
        here, from_east, from_west = ready
        if g + 1 < end:
            ready = turned(g + 1)
        p = PAD + 8 * g
        for j in range(COLUMNS):
            x = here[j]
            east = jnp.where(lane == LANES - 1, from_east[(j + 1) % COLUMNS], from_east[j])
            west = jnp.where(lane == 0, from_west[j - 1], from_west[j])
            south, north = src[j, p + 1 : p + 9, :], src[j, p - 1 : p + 7, :]
            rows = row_ref[j, p : p + 8, :] * (south - x) - row_ref[j, p - 1 : p + 7, :] * (x - north)
            cols = col_ref[j, p : p + 8, :] * (east - x) - west_ref[j, p : p + 8, :] * (x - west)
            dst[j, p : p + 8, :] = x + rows + cols


def ring(fields, left, right, picks):
    nrows = left.shape[0]
    lane = lax.broadcasted_iota(jnp.int32, (nrows, LANES), 1)

    def padded(k):
        after = pltpu.roll(right, LANES - k * HALO, 1) if k else right
        before = pltpu.roll(left, LANES - (k + 1) * HALO, 1)
        edge = jnp.where(lane < HALO, after, jnp.where(lane >= LANES - HALO, before, F32(0.0)))
        return jnp.concatenate([fields[k], edge], 1)

    made = {k: padded(k) for k in set(picks)}
    tiles, tail = [], None
    for f, k in enumerate(picks):
        part = pltpu.roll(made[k], 32 * f, 1) if f else made[k]
        begin = part[:, :LANES]
        tiles += [jnp.where(lane < 32 * f - HALO, tail, begin) if f else begin, part[:, LANES:256]]
        tail = part[:, 256:]
        wrap = tail if f == 0 else wrap
    return tiles + [jnp.where(lane < LANES - HALO, tail, wrap)]


def lay(fields, left, right, rows, a_ref, row_ref, col_ref):
    for ref, picks in ((a_ref, (0, 1, 2, 3)), (row_ref, (4,) * 4), (col_ref, (5,) * 4)):
        for j, tile in enumerate(ring(fields, left, right, picks)):
            ref[j, rows, :] = tile


def lay_west(col_ref, west_ref, rows):
    lane = lax.broadcasted_iota(jnp.int32, (rows.stop - rows.start, LANES), 1)
    for j in range(COLUMNS):
        before = pltpu.roll(col_ref[(j - 1) % COLUMNS, rows, :], 1, 1)
        west_ref[j, rows, :] = jnp.where(lane == 0, before, pltpu.roll(col_ref[j, rows, :], 1, 1))


def group(ref, g):
    return ref[:, PAD + 8 * g : PAD + 8 * g + 8, :]


def keep_and_sweep(first_ref, second_ref, row_ref, col_ref, west_ref, outer, top_ref, bottom_ref, count):
    def two(i, carry):
        for s, (src, dst) in enumerate(((first_ref, second_ref), (second_ref, first_ref))):
            top_ref[2 * i + s] = group(src, outer + 1)
            bottom_ref[2 * i + s] = group(src, 6 - outer)
            sweep(src, dst, row_ref, col_ref, west_ref, outer, 8 - outer)
        return carry

    lax.fori_loop(0, count // 2, two, 0)


def interior_first(
    own_ref, left_ref, right_ref, start_ref, row_ref, col_ref, west_ref, half_ref, top_ref, bottom_ref, other_ref
):
    own = slice(PAD, PAD + 64)
    for ref in (row_ref, half_ref, other_ref):
        ref[:, :PAD, :] = jnp.zeros((COLUMNS, PAD, LANES), F32)
        ref[:, PAD + 64 :, :] = jnp.zeros((COLUMNS, PAD, LANES), F32)
    lay([own_ref[k] for k in range(6)], left_ref[...], right_ref[...], own, start_ref, row_ref, col_ref)
    lay_west(col_ref, west_ref, own)
    half_ref[:, own, :] = start_ref[:, own, :]
    keep_and_sweep(half_ref, other_ref, row_ref, col_ref, west_ref, 0, top_ref, bottom_ref, EARLY)


def interior_second(
    quarter_ref, row_ref, col_ref, west_ref, sent_ref,
    top_mid, bottom_mid, half_ref, top_ref, bottom_ref, final_ref, a_ref, b_ref
):
    a_ref[...] = quarter_ref[...]
    b_ref[:, :PAD, :] = quarter_ref[:, :PAD, :]
    b_ref[:, PAD + 64 :, :] = quarter_ref[:, PAD + 64 :, :]
    keep_and_sweep(a_ref, b_ref, row_ref, col_ref, west_ref, 0, top_mid, bottom_mid, SWEEPS - EARLY)
    half_ref[0] = group(a_ref, 1)
    half_ref[1] = group(a_ref, 6)
    keep_and_sweep(a_ref, b_ref, row_ref, col_ref, west_ref, 1, top_ref, bottom_ref, SWEEPS)
    final_ref[...] = a_ref[:, PAD + 16 : PAD + 48, :]


def localize(
    scale_ref, above_ref, below_ref, left_ref, right_ref,
    own_ref, own_row, own_col, top_first, bottom_first, top_mid, bottom_mid, half_ref, top_second, bottom_second, final_ref,
    out_ref, a_ref, b_ref, row_ref, col_ref, west_ref,
):
    for ref in (a_ref, b_ref, row_ref):
        ref[:, :PAD, :] = jnp.zeros((COLUMNS, PAD, LANES), F32)
        ref[:, PAD + TALL :, :] = jnp.zeros((COLUMNS, PAD, LANES), F32)
    for side, (ref, begin) in enumerate(((above_ref, 0), (below_ref, TALL - HALO))):
        rows = slice(HALO * side, HALO * side + HALO)
        there = slice(PAD + begin, PAD + begin + HALO)
        fields = [ref[k] for k in range(6)]
        lay(fields, left_ref[rows, :], right_ref[rows, :], there, a_ref, row_ref, col_ref)
    for begin, end in ((0, 16), (40, 64)):
        here, there = slice(PAD + begin, PAD + end), slice(PAD + HALO + begin, PAD + HALO + end)
        row_ref[:, there, :] = own_row[:, here, :]
        col_ref[:, there, :] = own_col[:, here, :]
        a_ref[:, there, :] = own_ref[:, here, :]
    lay_west(col_ref, west_ref, slice(PAD, PAD + 32))
    lay_west(col_ref, west_ref, slice(PAD + 56, PAD + TALL))

    def put(ref, g, block):
        ref[:, PAD + 8 * g : PAD + 8 * g + 8, :] = block

    def several(outer, top_ref, bottom_ref, count):
        def two(i, carry):
            for s, (src, dst) in enumerate(((a_ref, b_ref), (b_ref, a_ref))):
                put(src, 3 + outer, top_ref[2 * i + s])
                put(src, 8 - outer, bottom_ref[2 * i + s])
                sweep(src, dst, row_ref, col_ref, west_ref, outer, 3 + outer)
                sweep(src, dst, row_ref, col_ref, west_ref, 9 - outer, GROUPS - outer)
            return carry

        lax.fori_loop(0, count // 2, two, 0)

    b_ref[:, PAD : PAD + 40, :] = a_ref[:, PAD : PAD + 40, :]
    b_ref[:, PAD + 56 : PAD + TALL, :] = a_ref[:, PAD + 56 : PAD + TALL, :]
    several(0, top_first, bottom_first, EARLY)
    several(0, top_mid, bottom_mid, SWEEPS - EARLY)
    put(a_ref, 3, half_ref[0])
    put(a_ref, 8, half_ref[1])
    several(1, top_second, bottom_second, SWEEPS)
    a_ref[:, PAD + 32 : PAD + 64, :] = final_ref[...]

    inner = slice(PAD + HALO, PAD + TALL - HALO)
    for c in range(2):
        total = None
        for m in range(2):
            f = 2 * m + c
            spread = jnp.concatenate([a_ref[2 * f + i, inner, :] for i in range(3)], 1)
            if f:
                spread = pltpu.roll(spread, 384 - 32 * f, 1)
            term = scale_ref[f] * spread[:, :256]
            total = term if total is None else total + term
        out_ref[2 * c] = total[:32]
        out_ref[2 * c + 1] = total[32:]


def local(vector, ensemble, diffusivity, norm_weight, static_var):
    tiles = lax.axis_size("tile")
    vmem = pl.BlockSpec(memory_space=pltpu.VMEM)
    hbm = pl.BlockSpec(memory_space=pltpu.HBM)
    params = pltpu.CompilerParams(vmem_limit_bytes=32 * 2**20)

    def f32(*shape):
        return jax.ShapeDtypeStruct(shape, F32)

    def buffers(*lead, rows):
        return [
            pltpu.VMEM((*lead, 2, rows, 256), F32), pltpu.VMEM((*lead, 2, 2, rows, 256), jnp.bfloat16),
            pltpu.VMEM((*lead, 2, rows, 256), F32), pltpu.VMEM((*lead, rows, 256), F32),
        ]

    held = [
        pltpu.with_memory_space_constraint(x, pltpu.HBM)
        for x in (vector, ensemble, diffusivity, norm_weight, static_var)
    ]
    first, last = pl.pallas_call(
        row_messages, out_shape=(f32(6, HALO, 256),) * 2, in_specs=[hbm] * 4, out_specs=(vmem,) * 2,
        scratch_shapes=buffers(2, rows=HALO) + [pltpu.SemaphoreType.DMA((8,))],
        compiler_params=params,
    )(*held[:4])
    down = [(i, i + COL_TILES) for i in range(tiles - COL_TILES)]
    up = [(b, a) for a, b in down]
    above = lax.ppermute(last, "tile", down)
    below = lax.ppermute(first, "tile", up)

    own, scale, fixed, first_own, last_own = pl.pallas_call(
        own_arrays,
        out_shape=(f32(6, 64, 256), f32(4, 64, 256), f32(2, 64, 256), f32(64, LANES), f32(64, LANES)),
        in_specs=[hbm] * 6, out_specs=(vmem,) * 5,
        scratch_shapes=buffers(rows=64) + [pltpu.VMEM((2, 64, 256), F32), pltpu.SemaphoreType.DMA((5,))],
        compiler_params=params,
        cost_estimate=pl.CostEstimate(flops=2 * 10**6, bytes_accessed=2 * 10**6, transcendentals=0),
    )(*held, first)

    rightward = [(i, i + 1) for i in range(tiles) if (i + 1) % COL_TILES]
    leftward = [(b, a) for a, b in rightward]
    left = lax.ppermute(last_own, "tile", rightward)
    right = lax.ppermute(first_own, "tile", leftward)

    rings = (COLUMNS, 64 + 2 * PAD, LANES)
    def edges(count):
        return (f32(count, COLUMNS, 8, LANES),) * 2

    start, row_ring, col_ring, west_ring, quarter, *first_edges = pl.pallas_call(
        interior_first,
        out_shape=(f32(*rings),) * 5 + edges(EARLY),
        in_specs=[vmem] * 3, out_specs=(vmem,) * 7,
        scratch_shapes=[pltpu.VMEM(rings, F32)],
        compiler_params=params,
        cost_estimate=pl.CostEstimate(flops=5 * 10**6, bytes_accessed=4 * 10**6, transcendentals=0),
    )(own, left, right)

    first, last = pl.pallas_call(
        corner_messages, out_shape=(f32(2 * HALO, LANES),) * 2, in_specs=[vmem] * 3, out_specs=(vmem,) * 2,
        compiler_params=params,
    )(above, below, quarter)
    left = lax.ppermute(last, "tile", rightward)
    right = lax.ppermute(first, "tile", leftward)
    second = pl.pallas_call(
        interior_second,
        out_shape=edges(SWEEPS - EARLY) + (f32(2, COLUMNS, 8, LANES),) + edges(SWEEPS) + (f32(COLUMNS, 32, LANES),),
        in_specs=[vmem] * 5, out_specs=(vmem,) * 6,
        scratch_shapes=[pltpu.VMEM(rings, F32)] * 2,
        compiler_params=params,
        cost_estimate=pl.CostEstimate(flops=5 * 10**6, bytes_accessed=4 * 10**6, transcendentals=0),
    )(quarter, row_ring, col_ring, west_ring, first)

    partial = pl.pallas_call(
        localize,
        out_shape=f32(4, 32, 256),
        in_specs=[vmem] * 16,
        out_specs=vmem,
        scratch_shapes=[pltpu.VMEM((COLUMNS, TALL + 2 * PAD, LANES), F32)] * 5,
        compiler_params=params,
    )(
        scale, above, below, left, right, start, row_ring, col_ring, *first_edges, *second
    )

    along_x = [[0, 1, 2, 3], [4, 5, 6, 7]]
    parts = lax.all_to_all(partial, "mem", 0, 0, axis_index_groups=along_x, tiled=True)
    mine = jnp.sum(parts, 0)
    pair = lax.all_gather(mine, "mem", axis_index_groups=[[0, 4], [1, 5], [2, 6], [3, 7]])
    both = jnp.broadcast_to((pair[0] + pair[1])[None], (4, 32, 256))
    summed = lax.all_to_all(both, "mem", 0, 0, axis_index_groups=along_x, tiled=True)
    members = lax.axis_size("mem") * ensemble.shape[0]
    ens_part = summed.reshape(2, 64, 256) / F32(members - 1)
    result = ens_weight * ens_part + fixed
    return result[:, None]


def solution(mesh):
    placed = (
        P(None, "tile", None, None),
        P("mem", None, "tile", None, None),
        P(None, "tile", None, None),
        P("tile", None, None),
        P(None, "tile", None, None),
    )
    return jax.shard_map(
        local, mesh=mesh, in_specs=placed, out_specs=P(None, "tile", None, None), check_vma=False
    )
```

```python
import jax
import jax.numpy as jnp
from jax import lax
from jax.experimental import pallas as pl
from jax.experimental.pallas import tpu as pltpu
from jax.sharding import PartitionSpec as P

COL_TILES = 8
SWEEPS = 8
HALO = 2 * SWEEPS
LANES = 128
FIELDS = 4
TALL = 64 + 2 * HALO
RING = FIELDS * (256 + 2 * HALO)
GROUPS = TALL // 8

ens_weight = 0.7
static_weight = 0.3

F32 = jnp.float32


def at_edges():
    tile_id, tiles = lax.axis_index("tile"), lax.axis_size("tile")
    return tile_id >= tiles - COL_TILES, tile_id % COL_TILES == COL_TILES - 1


def fetch(pairs, sems):
    copies = [pltpu.make_async_copy(src, dst, sems.at[i]) for i, (src, dst) in enumerate(pairs)]
    for copy in copies:
        copy.start()
    for copy in copies:
        copy.wait()


def row_messages(vec_hbm, ens_hbm, dif_hbm, weight_hbm, first_ref, last_ref, vec, ens, dif, weight, sems):
    nrows = vec_hbm.shape[2]
    pairs = []
    for side, begin in enumerate((0, nrows - HALO)):
        rows = pl.ds(begin, HALO)
        pairs += [
            (vec_hbm.at[:, 0, rows, :], vec.at[side]),
            (ens_hbm.at[:, :, 0, rows, :], ens.at[side]),
            (dif_hbm.at[:, 0, rows, :], dif.at[side]),
            (weight_hbm.at[0, rows, :], weight.at[side]),
        ]
    fetch(pairs, sems)
    bottom, rightmost = at_edges()
    row = lax.broadcasted_iota(jnp.int32, (HALO, 256), 0)
    col = lax.broadcasted_iota(jnp.int32, (HALO, 256), 1)
    for side, ref in enumerate((first_ref, last_ref)):
        for m in range(2):
            for c in range(2):
                ref[2 * m + c] = weight[side] * ens[side, m, c].astype(F32) * vec[side, c]
        row_coef, col_coef = dif[side, 0], dif[side, 1]
        if side == 1:
            row_coef = jnp.where((row == HALO - 1) & (bottom), F32(0.0), row_coef)
        ref[4] = row_coef
        ref[5] = jnp.where((col == 255) & (rightmost), F32(0.0), col_coef)


def pack_cols(fields):
    lane = lax.broadcasted_iota(jnp.int32, (fields[0].shape[0], LANES), 1)
    first = fields[0][:, :LANES]
    last = pltpu.roll(fields[0][:, -LANES:], HALO, 1)
    for k in range(1, 6):
        here = lane >= k * HALO
        first = jnp.where(here, pltpu.roll(fields[k][:, :LANES], k * HALO, 1), first)
        last = jnp.where(here, pltpu.roll(fields[k][:, -LANES:], (k + 1) * HALO, 1), last)
    return first, last


def own_arrays(
    vec_hbm, ens_hbm, dif_hbm, weight_hbm, var_hbm, sent_hbm,
    own_ref, scale_ref, fixed_ref, first_ref, last_ref, vec, ens, dif, weight, var, sems,
):
    fetch(
        [
            (vec_hbm.at[:, 0], vec), (ens_hbm.at[:, :, 0], ens), (dif_hbm.at[:, 0], dif),
            (weight_hbm.at[0], weight), (var_hbm.at[:, 0], var),
        ],
        sems,
    )
    nrows, ncols = weight.shape
    bottom, rightmost = at_edges()
    for m in range(2):
        for c in range(2):
            scale = weight[...] * ens[m, c].astype(F32)
            scale_ref[2 * m + c] = scale
            own_ref[2 * m + c] = scale * vec[c]
    row = lax.broadcasted_iota(jnp.int32, (nrows, ncols), 0)
    col = lax.broadcasted_iota(jnp.int32, (nrows, ncols), 1)
    own_ref[4] = jnp.where((row == nrows - 1) & (bottom), F32(0.0), dif[0])
    own_ref[5] = jnp.where((col == ncols - 1) & (rightmost), F32(0.0), dif[1])
    for c in range(2):
        fixed_ref[c] = F32(static_weight) * var[c] * vec[c]
    first_ref[...], last_ref[...] = pack_cols([own_ref[k] for k in range(6)])


def corner_messages(above_ref, below_ref, sent_ref, first_ref, last_ref):
    for side, ref in enumerate((above_ref, below_ref)):
        rows = slice(HALO * side, HALO * side + HALO)
        first_ref[rows, :], last_ref[rows, :] = pack_cols([ref[k] for k in range(6)])


EARLY = 4
PAD = 8
COLUMNS = RING // LANES


def sweep(src, dst, row_ref, col_ref, west_ref, begin, end):
    lane = lax.broadcasted_iota(jnp.int32, (8, LANES), 1)

    def turned(g):
        p = PAD + 8 * g
        here = [src[j, p : p + 8, :] for j in range(COLUMNS)]
        return here, [pltpu.roll(x, LANES - 1, 1) for x in here], [pltpu.roll(x, 1, 1) for x in here]

    ready = turned(begin)
    for g in range(begin, end):
        here, from_east, from_west = ready
        if g + 1 < end:
            ready = turned(g + 1)
        p = PAD + 8 * g
        for j in range(COLUMNS):
            x = here[j]
            east = jnp.where(lane == LANES - 1, from_east[(j + 1) % COLUMNS], from_east[j])
            west = jnp.where(lane == 0, from_west[j - 1], from_west[j])
            south, north = src[j, p + 1 : p + 9, :], src[j, p - 1 : p + 7, :]
            rows = row_ref[j, p : p + 8, :] * (south - x) - row_ref[j, p - 1 : p + 7, :] * (x - north)
            cols = col_ref[j, p : p + 8, :] * (east - x) - west_ref[j, p : p + 8, :] * (x - west)
            dst[j, p : p + 8, :] = x + rows + cols


def ring(fields, left, right, picks):
    nrows = left.shape[0]
    lane = lax.broadcasted_iota(jnp.int32, (nrows, LANES), 1)

    def padded(k):
        after = pltpu.roll(right, LANES - k * HALO, 1) if k else right
        before = pltpu.roll(left, LANES - (k + 1) * HALO, 1)
        edge = jnp.where(lane < HALO, after, jnp.where(lane >= LANES - HALO, before, F32(0.0)))
        return jnp.concatenate([fields[k], edge], 1)

    made = {k: padded(k) for k in set(picks)}
    tiles, tail = [], None
    for f, k in enumerate(picks):
        part = pltpu.roll(made[k], 32 * f, 1) if f else made[k]
        begin = part[:, :LANES]
        tiles += [jnp.where(lane < 32 * f - HALO, tail, begin) if f else begin, part[:, LANES:256]]
        tail = part[:, 256:]
        wrap = tail if f == 0 else wrap
    return tiles + [jnp.where(lane < LANES - HALO, tail, wrap)]


def lay(fields, left, right, rows, a_ref, row_ref, col_ref):
    for ref, picks in ((a_ref, (0, 1, 2, 3)), (row_ref, (4,) * 4), (col_ref, (5,) * 4)):
        for j, tile in enumerate(ring(fields, left, right, picks)):
            ref[j, rows, :] = tile


def lay_west(col_ref, west_ref, rows):
    lane = lax.broadcasted_iota(jnp.int32, (rows.stop - rows.start, LANES), 1)
    for j in range(COLUMNS):
        before = pltpu.roll(col_ref[(j - 1) % COLUMNS, rows, :], 1, 1)
        west_ref[j, rows, :] = jnp.where(lane == 0, before, pltpu.roll(col_ref[j, rows, :], 1, 1))


def group(ref, g):
    return ref[:, PAD + 8 * g : PAD + 8 * g + 8, :]


def keep_and_sweep(first_ref, second_ref, row_ref, col_ref, west_ref, outer, top_ref, bottom_ref, count):
    def two(i, carry):
        for s, (src, dst) in enumerate(((first_ref, second_ref), (second_ref, first_ref))):
            top_ref[2 * i + s] = group(src, outer + 1)
            bottom_ref[2 * i + s] = group(src, 6 - outer)
            sweep(src, dst, row_ref, col_ref, west_ref, outer, 8 - outer)
        return carry

    lax.fori_loop(0, count // 2, two, 0)


def interior_first(
    own_ref, left_ref, right_ref, start_ref, row_ref, col_ref, west_ref, half_ref, top_ref, bottom_ref, other_ref
):
    own = slice(PAD, PAD + 64)
    for ref in (row_ref, half_ref, other_ref):
        ref[:, :PAD, :] = jnp.zeros((COLUMNS, PAD, LANES), F32)
        ref[:, PAD + 64 :, :] = jnp.zeros((COLUMNS, PAD, LANES), F32)
    lay([own_ref[k] for k in range(6)], left_ref[...], right_ref[...], own, start_ref, row_ref, col_ref)
    lay_west(col_ref, west_ref, own)
    half_ref[:, own, :] = start_ref[:, own, :]
    keep_and_sweep(half_ref, other_ref, row_ref, col_ref, west_ref, 0, top_ref, bottom_ref, EARLY)


def interior_second(
    quarter_ref, row_ref, col_ref, west_ref, sent_ref,
    top_mid, bottom_mid, half_ref, top_ref, bottom_ref, final_ref, a_ref, b_ref
):
    a_ref[...] = quarter_ref[...]
    b_ref[:, :PAD, :] = quarter_ref[:, :PAD, :]
    b_ref[:, PAD + 64 :, :] = quarter_ref[:, PAD + 64 :, :]
    keep_and_sweep(a_ref, b_ref, row_ref, col_ref, west_ref, 0, top_mid, bottom_mid, SWEEPS - EARLY)
    half_ref[0] = group(a_ref, 1)
    half_ref[1] = group(a_ref, 6)
    keep_and_sweep(a_ref, b_ref, row_ref, col_ref, west_ref, 1, top_ref, bottom_ref, SWEEPS)
    final_ref[...] = a_ref[:, PAD + 16 : PAD + 48, :]


def localize(
    scale_ref, above_ref, below_ref, left_ref, right_ref,
    own_ref, own_row, own_col, top_first, bottom_first, top_mid, bottom_mid, half_ref, top_second, bottom_second, final_ref,
    out_ref, a_ref, b_ref, row_ref, col_ref, west_ref,
):
    def put(ref, g, block):
        ref[:, PAD + 8 * g : PAD + 8 * g + 8, :] = block

    for ref in (a_ref, b_ref, row_ref):
        ref[:, :PAD, :] = jnp.zeros((COLUMNS, PAD, LANES), F32)
        ref[:, PAD + TALL :, :] = jnp.zeros((COLUMNS, PAD, LANES), F32)
    for side, (ref, begin) in enumerate(((above_ref, 0), (below_ref, TALL - HALO))):
        rows = slice(HALO * side, HALO * side + HALO)
        there = slice(PAD + begin, PAD + begin + HALO)
        fields = [ref[k] for k in range(6)]
        lay(fields, left_ref[rows, :], right_ref[rows, :], there, a_ref, row_ref, col_ref)
    for begin, end in ((0, 16), (40, 64)):
        here, there = slice(PAD + begin, PAD + end), slice(PAD + HALO + begin, PAD + HALO + end)
        row_ref[:, there, :] = own_row[:, here, :]
        col_ref[:, there, :] = own_col[:, here, :]
    for g in (0, 7):
        put(a_ref, g + 2, group(own_ref, g))
    lay_west(col_ref, west_ref, slice(PAD, PAD + 32))
    lay_west(col_ref, west_ref, slice(PAD + 56, PAD + TALL))

    def several(outer, top_ref, bottom_ref, count):
        def two(i, carry):
            for s, (src, dst) in enumerate(((a_ref, b_ref), (b_ref, a_ref))):
                put(src, 3 + outer, top_ref[2 * i + s])
                put(src, 8 - outer, bottom_ref[2 * i + s])
                sweep(src, dst, row_ref, col_ref, west_ref, outer, 3 + outer)
                sweep(src, dst, row_ref, col_ref, west_ref, 9 - outer, GROUPS - outer)
            return carry

        lax.fori_loop(0, count // 2, two, 0)

    several(0, top_first, bottom_first, EARLY)
    several(0, top_mid, bottom_mid, SWEEPS - EARLY)
    put(a_ref, 3, half_ref[0])
    put(a_ref, 8, half_ref[1])
    several(1, top_second, bottom_second, SWEEPS)
    a_ref[:, PAD + 32 : PAD + 64, :] = final_ref[...]

    inner = slice(PAD + HALO, PAD + TALL - HALO)
    for c in range(2):
        total = None
        for m in range(2):
            f = 2 * m + c
            spread = jnp.concatenate([a_ref[2 * f + i, inner, :] for i in range(3)], 1)
            if f:
                spread = pltpu.roll(spread, 384 - 32 * f, 1)
            term = scale_ref[f] * spread[:, :256]
            total = term if total is None else total + term
        out_ref[2 * c] = total[:32]
        out_ref[2 * c + 1] = total[32:]


def local(vector, ensemble, diffusivity, norm_weight, static_var):
    tiles = lax.axis_size("tile")
    vmem = pl.BlockSpec(memory_space=pltpu.VMEM)
    hbm = pl.BlockSpec(memory_space=pltpu.HBM)
    params = pltpu.CompilerParams(vmem_limit_bytes=32 * 2**20)

    def f32(*shape):
        return jax.ShapeDtypeStruct(shape, F32)

    def buffers(*lead, rows):
        return [
            pltpu.VMEM((*lead, 2, rows, 256), F32), pltpu.VMEM((*lead, 2, 2, rows, 256), jnp.bfloat16),
            pltpu.VMEM((*lead, 2, rows, 256), F32), pltpu.VMEM((*lead, rows, 256), F32),
        ]

    held = [
        pltpu.with_memory_space_constraint(x, pltpu.HBM)
        for x in (vector, ensemble, diffusivity, norm_weight, static_var)
    ]
    first, last = pl.pallas_call(
        row_messages, out_shape=(f32(6, HALO, 256),) * 2, in_specs=[hbm] * 4, out_specs=(vmem,) * 2,
        scratch_shapes=buffers(2, rows=HALO) + [pltpu.SemaphoreType.DMA((8,))],
        compiler_params=params,
    )(*held[:4])
    down = [(i, i + COL_TILES) for i in range(tiles - COL_TILES)]
    up = [(b, a) for a, b in down]
    above = lax.ppermute(last, "tile", down)
    below = lax.ppermute(first, "tile", up)

    own, scale, fixed, first_own, last_own = pl.pallas_call(
        own_arrays,
        out_shape=(f32(6, 64, 256), f32(4, 64, 256), f32(2, 64, 256), f32(64, LANES), f32(64, LANES)),
        in_specs=[hbm] * 6, out_specs=(vmem,) * 5,
        scratch_shapes=buffers(rows=64) + [pltpu.VMEM((2, 64, 256), F32), pltpu.SemaphoreType.DMA((5,))],
        compiler_params=params,
        cost_estimate=pl.CostEstimate(flops=2 * 10**6, bytes_accessed=2 * 10**6, transcendentals=0),
    )(*held, first)

    rightward = [(i, i + 1) for i in range(tiles) if (i + 1) % COL_TILES]
    leftward = [(b, a) for a, b in rightward]
    left = lax.ppermute(last_own, "tile", rightward)
    right = lax.ppermute(first_own, "tile", leftward)

    rings = (COLUMNS, 64 + 2 * PAD, LANES)
    def edges(count):
        return (f32(count, COLUMNS, 8, LANES),) * 2

    start, row_ring, col_ring, west_ring, quarter, *first_edges = pl.pallas_call(
        interior_first,
        out_shape=(f32(*rings),) * 5 + edges(EARLY),
        in_specs=[vmem] * 3, out_specs=(vmem,) * 7,
        scratch_shapes=[pltpu.VMEM(rings, F32)],
        compiler_params=params,
        cost_estimate=pl.CostEstimate(flops=5 * 10**6, bytes_accessed=4 * 10**6, transcendentals=0),
    )(own, left, right)

    first, last = pl.pallas_call(
        corner_messages, out_shape=(f32(2 * HALO, LANES),) * 2, in_specs=[vmem] * 3, out_specs=(vmem,) * 2,
        compiler_params=params,
    )(above, below, quarter)
    left = lax.ppermute(last, "tile", rightward)
    right = lax.ppermute(first, "tile", leftward)
    second = pl.pallas_call(
        interior_second,
        out_shape=edges(SWEEPS - EARLY) + (f32(2, COLUMNS, 8, LANES),) + edges(SWEEPS) + (f32(COLUMNS, 32, LANES),),
        in_specs=[vmem] * 5, out_specs=(vmem,) * 6,
        scratch_shapes=[pltpu.VMEM(rings, F32)] * 2,
        compiler_params=params,
        cost_estimate=pl.CostEstimate(flops=5 * 10**6, bytes_accessed=4 * 10**6, transcendentals=0),
    )(quarter, row_ring, col_ring, west_ring, first)

    partial = pl.pallas_call(
        localize,
        out_shape=f32(4, 32, 256),
        in_specs=[vmem] * 16,
        out_specs=vmem,
        scratch_shapes=[pltpu.VMEM((COLUMNS, TALL + 2 * PAD, LANES), F32)] * 5,
        compiler_params=params,
    )(
        scale, above, below, left, right, start, row_ring, col_ring, *first_edges, *second
    )

    along_x = [[0, 1, 2, 3], [4, 5, 6, 7]]
    parts = lax.all_to_all(partial, "mem", 0, 0, axis_index_groups=along_x, tiled=True)
    mine = jnp.sum(parts, 0)
    pair = lax.all_gather(mine, "mem", axis_index_groups=[[0, 4], [1, 5], [2, 6], [3, 7]])
    both = jnp.broadcast_to((pair[0] + pair[1])[None], (4, 32, 256))
    summed = lax.all_to_all(both, "mem", 0, 0, axis_index_groups=along_x, tiled=True)
    members = lax.axis_size("mem") * ensemble.shape[0]
    ens_part = summed.reshape(2, 64, 256) / F32(members - 1)
    result = ens_weight * ens_part + fixed
    return result[:, None]


def solution(mesh):
    placed = (
        P(None, "tile", None, None),
        P("mem", None, "tile", None, None),
        P(None, "tile", None, None),
        P("tile", None, None),
        P(None, "tile", None, None),
    )
    return jax.shard_map(
        local, mesh=mesh, in_specs=placed, out_specs=P(None, "tile", None, None), check_vma=False
    )
```
